256 devices in a mesh: ctx: 16 (over y_hi, z), head: 16 (over y_lo, x, core).
Axes of the slice: x: 4, y: 4 (y_hi: 2, y_lo: 2; y = y_hi * 2 + y_lo), z: 8, core: 2. Of those that a mesh axis runs over, the one named last changes fastest.
Arguments:
- key_rows: bfloat16 [32768, 4096], P('ctx', 'head'), may hold values from -4 to 4
- query_rows: bfloat16 [32768, 4096], P('ctx', 'head'), may hold values from -4 to 4
- row_lse: bfloat16 [32, 32768], P('head', 'ctx'), may hold values from 10.5 to 12.5
- query_offsets: int32 [32768], P('ctx'), may hold values from 0 to 2047
Outputs:
- key_mass: float32 [32768], P(('ctx', 'head'))
The draws below stay inside these ranges and needn't reach their ends.
All inputs are finite; a program needn't handle non-finite values.
Results may differ from the reference program's by a relative error of at most 0.0003.
Values may be sent and summed in bfloat16 or wider, within the bound.
No kernel may reach another device: no remote copies, remote signals or barrier semaphores. Data moves between devices by JAX's collectives and lax.ppermute only.
A program may use at most 64 MiB of HBM per device.

```python
import jax
import jax.numpy as jnp
from jax import lax

HEADS = 32
HD = 128
KEYS_DEV = 2048
QROWS = 2048
CONTEXT = 32768
QUERIES = 32768
N_CTX = 16


def shared_keys(key):
    values = jax.random.normal(key, (CONTEXT, HEADS, HD), jnp.float32)
    return jnp.clip(values, -4.0, 4.0)


def copied_queries(keys, key, noise, low_strength, high_strength):
    first, second, third, fourth, fifth = jax.random.split(key, 5)
    rows = jnp.arange(QUERIES, dtype=jnp.int32)
    own_block = rows // QROWS
    distance = jax.random.randint(first, (QUERIES, HEADS), 1, 4)
    target_block = jnp.maximum(own_block[:, None] - distance, 0)
    slot = jax.random.randint(second, (QUERIES, HEADS), 0, 512)
    hitters = jax.random.randint(third, (CONTEXT // KEYS_DEV, 512, HEADS), 0, KEYS_DEV)
    head_index = jnp.arange(HEADS, dtype=jnp.int32)[None, :]
    chosen = hitters[target_block, slot, head_index]
    position = target_block * KEYS_DEV + chosen
    target = keys[position, head_index]
    copies = jax.random.randint(fourth, (QUERIES, HEADS), 0, 20) == 0
    strength = jax.random.uniform(fifth, (QUERIES, HEADS, 1), jnp.float32, low_strength, high_strength)
    copied = strength * target + 0.5 * noise
    values = jnp.where(copies[:, :, None], copied, noise)
    return jnp.clip(values, -4.0, 4.0)


def draw_key_rows(key, part):
    keys = shared_keys(key)
    return keys.reshape(CONTEXT, HEADS * HD).astype(jnp.bfloat16)


def draw_query_rows(key, part):
    keys = shared_keys(key)
    key = jax.random.fold_in(key, 2)
    noise_key, pick_key = jax.random.split(key)
    noise = jax.random.normal(noise_key, (QUERIES, HEADS, HD), jnp.float32)
    values = copied_queries(keys, pick_key, noise, 0.65, 1.15)
    return values.reshape(QUERIES, HEADS * HD).astype(jnp.bfloat16)


def place_ends(values, rng, low, high):
    longest = values.shape.index(max(values.shape))
    spots = []
    for shift in (0, 1):
        where = [jax.random.randint(jax.random.fold_in(rng, axis), (), 0, length) for axis, length in enumerate(values.shape)]
        where[longest] = (where[longest] + shift) % values.shape[longest]
        spots.append(tuple(where))
    return values.at[spots[0]].set(low).at[spots[1]].set(high)


def steps_of(own_key, shape, shards, least, top_value):
    level = 1.0
    for dim, shards_of in shards:
        steps = jax.random.uniform(jax.random.fold_in(jax.random.fold_in(own_key, 6), dim), (shards_of,), jnp.float32, least / len(shards), top_value / len(shards))
        level = level * jnp.repeat(jnp.exp(steps), shape[dim] // shards_of).reshape((-1,) + (1,) * (len(shape) - 1 - dim))
    return level


def setup_inputs(seed: int = 0) -> dict:
    seeds = jax.random.split(jax.random.key(seed), 5)
    key_rows = draw_key_rows(jax.random.fold_in(seeds[4], 71), 0)
    query_rows = draw_query_rows(jax.random.fold_in(seeds[4], 71), 0)
    row_lse = jnp.clip(10.5 + 2.0 * jax.random.uniform(seeds[2], (HEADS, QUERIES), jnp.float32) ** steps_of(seeds[2], (HEADS, QUERIES), ((0, 16), (1, 16)), -0.2, 0.2), 10.5, 12.5).astype(jnp.bfloat16)
    query_offsets = place_ends(jax.random.randint(seeds[3], (QUERIES,), 0, KEYS_DEV), jax.random.fold_in(seeds[3], 1), 0, KEYS_DEV - 1).astype(jnp.int32)
    return {"key_rows": key_rows, "query_rows": query_rows, "row_lse": row_lse, "query_offsets": query_offsets}


def reference(key_rows, query_rows, row_lse, query_offsets):
    softmax_scale = 1.0 / (HD ** 0.5)
    key_blocks = key_rows.reshape(N_CTX, KEYS_DEV, HEADS, HD)
    query_blocks = query_rows.reshape(N_CTX, QROWS, HEADS, HD)
    lse_blocks = row_lse.reshape(HEADS, N_CTX, QROWS)
    offset_blocks = query_offsets.reshape(N_CTX, QROWS)
    key_index = jnp.arange(KEYS_DEV, dtype=jnp.int32)

    def one_block(block_index):
        key_block = lax.dynamic_index_in_dim(key_blocks, block_index, 0, keepdims=False).astype(jnp.float32)
        running = jnp.zeros((KEYS_DEV,), jnp.float32)
        for distance in range(4):
            source = block_index + distance
            clipped = jnp.minimum(source, N_CTX - 1).astype(jnp.int32)
            query_block = lax.dynamic_index_in_dim(query_blocks, clipped, 0, keepdims=False).astype(jnp.float32)
            lse_block = lax.dynamic_index_in_dim(lse_blocks, clipped, 1, keepdims=False).astype(jnp.float32)
            offsets = lax.dynamic_index_in_dim(offset_blocks, clipped, 0, keepdims=False)
            scores = jnp.einsum("qhd,khd->hqk", query_block, key_block) * softmax_scale
            weights = jnp.exp(scores - lse_block[:, :, None])
            if distance == 0:
                allowed = key_index[None, :] <= offsets[:, None]
            else:
                allowed = jnp.ones((QROWS, KEYS_DEV), bool)
            allowed = jnp.logical_and(allowed, source < N_CTX)
            running = running + jnp.sum(jnp.where(allowed[None], weights, 0.0), axis=(0, 1))
        return running

    masses = lax.map(one_block, jnp.arange(N_CTX, dtype=jnp.int32))
    return masses.reshape(-1)
```

```python
import functools
import math

import jax
import jax.numpy as jnp
from jax import lax
from jax.experimental import pallas as pl
from jax.experimental.pallas import tpu as pltpu
from jax.sharding import PartitionSpec as P

HD = 128
LANES = 128
LOG2E = math.log2(math.e)
SCORE_SCALE = LOG2E / math.sqrt(HD)
DEAD = 1e30
Q_TILE = 256
CONTRACT_LAST = (((1,), (1,)), ((), ()))
VMEM_LIMIT = 40 * 2**20


def role_of_device():
    return lax.rem(lax.axis_index("head"), 2)


def prepare_kernel(q_ref, k_ref, lse_ref, x_ref, za_ref, zb_ref, lse_wide, lse_rows, sems):
    rows = q_ref.shape[0]
    lse_count = rows // LANES
    role = role_of_device()

    def arrange(moving, fixed):
        copies = [
            pltpu.make_async_copy(moving.at[:, :HD], x_ref.at[:rows], sems.at[0]),
            pltpu.make_async_copy(moving.at[:, HD:], x_ref.at[rows : 2 * rows], sems.at[1]),
            pltpu.make_async_copy(fixed.at[:, :HD], za_ref.at[:rows], sems.at[2]),
            pltpu.make_async_copy(fixed.at[:, HD:], zb_ref.at[:rows], sems.at[3]),
        ]
        for copy in copies:
            copy.start()
        lse_wide[...] = lse_ref[...].astype(jnp.float32)
        wide = []
        for head in range(2):
            for part in range(lse_count):
                wide.append(lse_wide[head : head + 1, part * LANES : (part + 1) * LANES])
        lse_rows[...] = jnp.concatenate(wide, axis=0).astype(jnp.bfloat16)
        small = [
            pltpu.make_async_copy(lse_rows, x_ref.at[2 * rows :], sems.at[4]),
            pltpu.make_async_copy(lse_rows.at[:lse_count], za_ref.at[rows:], sems.at[5]),
            pltpu.make_async_copy(lse_rows.at[lse_count:], zb_ref.at[rows:], sems.at[6]),
        ]
        for copy in small:
            copy.start()
        for copy in copies + small:
            copy.wait()

    pl.when(role == 0)(lambda: arrange(q_ref, k_ref))
    pl.when(role == 1)(lambda: arrange(k_ref, q_ref))


def prepare(key_rows, query_rows, row_lse):
    rows = query_rows.shape[0]
    lse_count = rows // LANES
    return pl.pallas_call(
        prepare_kernel,
        out_shape=(
            jax.ShapeDtypeStruct((2 * (rows + lse_count), HD), jnp.bfloat16),
            jax.ShapeDtypeStruct((rows + lse_count, HD), jnp.bfloat16),
            jax.ShapeDtypeStruct((rows + lse_count, HD), jnp.bfloat16),
        ),
        in_specs=[
            pl.BlockSpec(memory_space=pl.ANY),
            pl.BlockSpec(memory_space=pl.ANY),
            pl.BlockSpec(memory_space=pltpu.VMEM),
        ],
        out_specs=(pl.BlockSpec(memory_space=pl.ANY),) * 3,
        scratch_shapes=[
            pltpu.VMEM((2, rows), jnp.float32),
            pltpu.VMEM((2 * lse_count, LANES), jnp.bfloat16),
            pltpu.SemaphoreType.DMA((7,)),
        ],
        compiler_params=pltpu.CompilerParams(vmem_limit_bytes=VMEM_LIMIT),
        name="prepare",
    )(query_rows, key_rows, row_lse)


def add_pair(q_buf, k_buf, lse_buf, offsets, acc, is_first, is_live):
    rows = k_buf.shape[0]
    lse = lse_buf[...].astype(jnp.float32) * LOG2E
    lse = jnp.where(is_live, lse, DEAD)
    parts = Q_TILE // LANES
    for tile in range(q_buf.shape[0] // Q_TILE):
        scores = lax.dot_general(
            k_buf[...],
            q_buf[tile * Q_TILE : (tile + 1) * Q_TILE, :],
            CONTRACT_LAST,
            preferred_element_type=jnp.float32,
        )
        total = None
        for part in range(parts):
            row = tile * parts + part
            weights = jnp.exp2(
                scores[:, part * LANES : (part + 1) * LANES] * SCORE_SCALE - lse[row : row + 1, :]
            )
            if offsets is not None:
                key_index = lax.broadcasted_iota(jnp.int32, (rows, LANES), 0)
                weights = jnp.where(key_index <= offsets[row : row + 1, :], weights, 0.0)
            total = weights if total is None else total + weights
        if is_first and tile == 0:
            acc[...] = total
        else:
            acc[...] += total


def write_mass(acc, out_ref):
    for part in range(out_ref.shape[0]):
        turned = acc[part * LANES : (part + 1) * LANES, :].T
        out_ref[part : part + 1, :] = jnp.sum(turned, axis=0, keepdims=True)


def mass_kernel(jobs, n_arrays, n_small, finish, has_offsets, *refs):
    arrays = refs[:n_arrays]
    small = refs[n_arrays : n_arrays + n_small]
    n_out = 1 + max(job["out"] for job in jobs) if finish is None else 2
    outs = refs[n_arrays + n_small : n_arrays + n_small + n_out]
    q_buf, k_buf, lse_buf, acc, sems = refs[n_arrays + n_small + n_out :]
    rows = q_buf.shape[1]
    lse_count = lse_buf.shape[1]
    role = role_of_device()
    shard = lax.axis_index("ctx")
    shards = lax.axis_size("ctx")

    def copies_of(number, x_is_query):
        job = jobs[number]
        x, z = arrays[job["x"]], arrays[job["z"]]
        x_at, z_at = job["x_head"] * rows, job["z_head"] * rows
        x_lse = 2 * rows + job["x_head"] * lse_count if x.shape[0] > 2 * rows else rows
        z_lse = 2 * rows + job["z_head"] * lse_count if z.shape[0] > 2 * rows else rows
        query, q_at, lse_at, key, k_at = (
            (x, x_at, x_lse, z, z_at) if x_is_query else (z, z_at, z_lse, x, x_at)
        )
        return [
            pltpu.make_async_copy(key.at[pl.ds(k_at, rows)], k_buf.at[number], sems.at[number, 0]),
            pltpu.make_async_copy(
                query.at[pl.ds(q_at, rows)], q_buf.at[number], sems.at[number, 1]
            ),
            pltpu.make_async_copy(
                query.at[pl.ds(lse_at, lse_count)], lse_buf.at[number], sems.at[number, 2]
            ),
        ]

    def start_all(x_is_query):
        for number in range(len(jobs)):
            for copy in copies_of(number, x_is_query):
                copy.start()

    pl.when(role == 0)(lambda: start_all(True))
    pl.when(role == 1)(lambda: start_all(False))
    seen = set()
    for number, job in enumerate(jobs):
        for copy in copies_of(number, True):
            copy.wait()
        steps = jnp.where(role == 0, job["x_steps"], job["z_steps"])
        add_pair(
            q_buf.at[number],
            k_buf.at[number],
            lse_buf.at[number],
            small[0][...] if has_offsets else None,
            acc,
            job["out"] not in seen,
            shard + steps < shards,
        )
        seen.add(job["out"])
        if number + 1 == len(jobs) or jobs[number + 1]["out"] != job["out"]:
            write_mass(acc, outs[job["out"]])
    if finish is not None:
        finish(role, small, outs)


def mass_call(name, arrays, jobs, small=(), finish=None, has_offsets=False):
    rows = 2048 if not arrays else arrays[-1].shape[0] * LANES // (LANES + 1)
    lse_count = rows // LANES
    n_out = 1 + max(job["out"] for job in jobs) if finish is None else 2
    pairs = len(jobs) * rows * rows
    return pl.pallas_call(
        functools.partial(mass_kernel, jobs, len(arrays), len(small), finish, has_offsets),
        out_shape=tuple(
            jax.ShapeDtypeStruct((lse_count, LANES), jnp.float32) for _ in range(n_out)
        ),
        in_specs=[pl.BlockSpec(memory_space=pl.ANY)] * len(arrays)
        + [pl.BlockSpec(memory_space=pltpu.VMEM)] * len(small),
        out_specs=tuple(pl.BlockSpec(memory_space=pltpu.VMEM) for _ in range(n_out)),
        scratch_shapes=[
            pltpu.VMEM((len(jobs), rows, HD), jnp.bfloat16),
            pltpu.VMEM((len(jobs), rows, HD), jnp.bfloat16),
            pltpu.VMEM((len(jobs), lse_count, LANES), jnp.bfloat16),
            pltpu.VMEM((rows, LANES), jnp.float32),
            pltpu.SemaphoreType.DMA((len(jobs), 3)),
        ],
        compiler_params=pltpu.CompilerParams(vmem_limit_bytes=VMEM_LIMIT),
        cost_estimate=pl.CostEstimate(
            flops=2 * pairs * HD, transcendentals=pairs, bytes_accessed=len(jobs) * 2**20
        ),
        name=name,
    )(*arrays, *small)


def job(x, x_head, x_steps, z, z_head, z_steps, out=0):
    return dict(x=x, x_head=x_head, x_steps=x_steps, z=z, z_head=z_head, z_steps=z_steps, out=out)


def combine(role, small, outs):
    own, first, first_back, second, third = [ref[...] for ref in small]
    last = outs[0][...] + third
    is_query_mover = role == 0
    outs[0][...] = jnp.where(is_query_mover, last, last + second)
    outs[1][...] = own + first_back + jnp.where(is_query_mover, first + second, 0.0)


def move(value, mesh_shape, steps_of_role):
    shards, heads = mesh_shape
    pairs = []
    for shard in range(shards):
        for head in range(heads):
            steps = steps_of_role[head % 2]
            if steps != 0 and 0 <= shard + steps < shards:
                pairs.append((shard * heads + head, (shard + steps) * heads + head))
    return lax.ppermute(value, ("ctx", "head"), pairs)


def on_device(mesh_shape, key_rows, query_rows, row_lse, query_offsets):
    rows = query_rows.shape[0]
    x0, za0, zb0 = prepare(key_rows, query_rows, row_lse)
    x1 = move(x0, mesh_shape, (-1, 1))
    za1 = move(za0, mesh_shape, (1, -1))
    offsets = query_offsets.reshape(rows // LANES, LANES)
    (own,) = mass_call(
        "own",
        [x0, za0, zb0],
        [job(0, 0, 0, 1, 0, 0), job(0, 1, 0, 2, 0, 0)],
        small=(offsets,),
        has_offsets=True,
    )
    x1, own = lax.optimization_barrier((x1, own))
    x2 = move(x1, mesh_shape, (-1, 1))
    za1, x1 = lax.optimization_barrier((za1, x1))
    (first,) = mass_call(
        "first", [x1, za0, zb0], [job(0, 0, 1, 1, 0, 0), job(0, 1, 1, 2, 0, 0)]
    )
    first_back = move(first, mesh_shape, (0, -1))
    zb0, first = lax.optimization_barrier((zb0, first))
    zb1 = move(zb0, mesh_shape, (1, -1))
    second, third = mass_call(
        "second",
        [x2, za0, zb0, za1],
        [job(0, 0, 2, 1, 0, 0), job(0, 1, 2, 2, 0, 0), job(0, 0, 2, 3, 0, 1, out=1)],
    )
    back, local = mass_call(
        "third",
        [x2, zb1],
        [job(0, 1, 2, 1, 0, 1)],
        small=(own, first, first_back, second, third),
        finish=combine,
    )
    local = local + move(back, mesh_shape, (-1, -2))
    spread = lax.all_to_all(local, "head", 0, 0, tiled=True)
    return jnp.sum(spread, axis=0)


def solution(mesh):
    mesh_shape = (mesh.shape["ctx"], mesh.shape["head"])
    in_specs = (P("ctx", "head"), P("ctx", "head"), P("head", "ctx"), P("ctx"))
    out_specs = P(("ctx", "head"))
    return jax.shard_map(
        functools.partial(on_device, mesh_shape),
        mesh=mesh,
        in_specs=in_specs,
        out_specs=out_specs,
        check_vma=False,
    )
```

```python
import functools
import math

import jax
import jax.numpy as jnp
from jax import lax
from jax.experimental import pallas as pl
from jax.experimental.pallas import tpu as pltpu
from jax.sharding import PartitionSpec as P

HD = 128
LANES = 128
LOG2E = math.log2(math.e)
SCORE_SCALE = LOG2E / math.sqrt(HD)
DEAD = 1e30
Q_TILE = 256
CONTRACT_LAST = (((1,), (1,)), ((), ()))
VMEM_LIMIT = 40 * 2**20


def role_of_device():
    return lax.rem(lax.axis_index("head"), 2)


def prepare_kernel(q_ref, k_ref, lse_ref, xa_ref, xb_ref, za_ref, zb_ref, lse_rows, sems):
    rows = q_ref.shape[0]
    lse_count = rows // LANES
    role = role_of_device()

    def arrange(moving, fixed):
        copies = [
            pltpu.make_async_copy(moving.at[:, :HD], xa_ref.at[:rows], sems.at[0]),
            pltpu.make_async_copy(moving.at[:, HD:], xb_ref.at[:rows], sems.at[1]),
            pltpu.make_async_copy(fixed.at[:, :HD], za_ref.at[:rows], sems.at[2]),
            pltpu.make_async_copy(fixed.at[:, HD:], zb_ref.at[:rows], sems.at[3]),
        ]
        for copy in copies:
            copy.start()
        lse = lse_ref[...].astype(jnp.float32)
        for head in range(2):
            pieces = [
                lse[head : head + 1, part * LANES : (part + 1) * LANES]
                for part in range(lse_count)
            ]
            lse_rows[head] = jnp.concatenate(pieces, axis=0).astype(jnp.bfloat16)
        for number, (ref, head) in enumerate(
            [(xa_ref, 0), (xb_ref, 1), (za_ref, 0), (zb_ref, 1)]
        ):
            copies.append(
                pltpu.make_async_copy(lse_rows.at[head], ref.at[rows:], sems.at[4 + number])
            )
            copies[-1].start()
        for copy in copies:
            copy.wait()

    pl.when(role == 0)(lambda: arrange(q_ref, k_ref))
    pl.when(role == 1)(lambda: arrange(k_ref, q_ref))


def prepare(key_rows, query_rows, row_lse):
    rows = query_rows.shape[0]
    lse_count = rows // LANES
    half = jax.ShapeDtypeStruct((rows + lse_count, HD), jnp.bfloat16)
    return pl.pallas_call(
        prepare_kernel,
        out_shape=(half,) * 4,
        in_specs=[
            pl.BlockSpec(memory_space=pltpu.HBM),
            pl.BlockSpec(memory_space=pltpu.HBM),
            pl.BlockSpec(memory_space=pltpu.VMEM),
        ],
        out_specs=(pl.BlockSpec(memory_space=pl.ANY),) * 4,
        scratch_shapes=[
            pltpu.VMEM((2, lse_count, LANES), jnp.bfloat16),
            pltpu.SemaphoreType.DMA((8,)),
        ],
        compiler_params=pltpu.CompilerParams(vmem_limit_bytes=VMEM_LIMIT),
        name="prepare",
    )(
        pltpu.with_memory_space_constraint(query_rows, pltpu.HBM),
        pltpu.with_memory_space_constraint(key_rows, pltpu.HBM),
        row_lse,
    )


def add_pair(q_buf, k_buf, lse_buf, offsets, key_index, acc, is_first, is_live):
    lse = lse_buf[...].astype(jnp.float32) * LOG2E
    lse = jnp.where(is_live, lse, DEAD)
    parts = Q_TILE // LANES
    for tile in range(q_buf.shape[0] // Q_TILE):
        scores = lax.dot_general(
            k_buf[...],
            q_buf[tile * Q_TILE : (tile + 1) * Q_TILE, :],
            CONTRACT_LAST,
            preferred_element_type=jnp.float32,
        )
        total = None
        for part in range(parts):
            row = tile * parts + part
            weights = jnp.exp2(
                scores[:, part * LANES : (part + 1) * LANES] * SCORE_SCALE - lse[row : row + 1, :]
            )
            if offsets is not None:
                weights = jnp.where(key_index[...] <= offsets[row : row + 1, :], weights, 0.0)
            total = weights if total is None else total + weights
        if is_first and tile == 0:
            acc[...] = total
        else:
            acc[...] += total


def turned_mass(acc, count):
    parts = []
    for part in range(count):
        turned = acc[part * LANES : (part + 1) * LANES, :].T
        parts.append(jnp.sum(turned, axis=0, keepdims=True))
    return jnp.concatenate(parts, axis=0)


def mass_kernel(jobs, n_arrays, n_small, n_out, finish, is_own, *refs):
    arrays = refs[:n_arrays]
    small = refs[n_arrays : n_arrays + n_small]
    outs = refs[n_arrays + n_small : n_arrays + n_small + n_out]
    q_buf, k_buf, lse_buf, acc, key_index, sems = refs[n_arrays + n_small + n_out :]
    rows = q_buf.shape[1]
    lse_count = lse_buf.shape[1]
    role = role_of_device()
    shard = lax.axis_index("ctx")
    shards = lax.axis_size("ctx")

    def copies_of(number, x_is_query):
        x, z = arrays[jobs[number]["x"]], arrays[jobs[number]["z"]]
        query, key = (x, z) if x_is_query else (z, x)
        return [
            pltpu.make_async_copy(key.at[:rows], k_buf.at[number], sems.at[number, 0]),
            pltpu.make_async_copy(query.at[:rows], q_buf.at[number], sems.at[number, 1]),
            pltpu.make_async_copy(query.at[rows:], lse_buf.at[number], sems.at[number, 2]),
        ]

    def start_all(x_is_query):
        for number in range(len(jobs)):
            for copy in copies_of(number, x_is_query):
                copy.start()

    pl.when(role == 0)(lambda: start_all(True))
    pl.when(role == 1)(lambda: start_all(False))
    if is_own:
        key_index[...] = lax.broadcasted_iota(jnp.int32, key_index.shape, 0)
    masses = {}
    for number, job in enumerate(jobs):
        for copy in copies_of(number, True):
            copy.wait()
        steps = jnp.where(role == 0, job["x_steps"], job["z_steps"])
        add_pair(
            q_buf.at[number],
            k_buf.at[number],
            lse_buf.at[number],
            small[0][...] if is_own else None,
            key_index,
            acc,
            job["out"] not in masses,
            shard + steps < shards,
        )
        masses[job["out"]] = None
        if number + 1 == len(jobs) or jobs[number + 1]["out"] != job["out"]:
            masses[job["out"]] = turned_mass(acc, lse_count)
    results = [masses[number] for number in sorted(masses)]
    if finish is not None:
        results = finish(role, results, [ref[...] for ref in small])
    for out, result in zip(outs, results):
        out[...] = result


def mass_call(name, arrays, jobs, small=(), n_out=1, finish=None, is_own=False):
    padded = arrays[0].shape[0]
    rows = padded * LANES // (LANES + 1)
    lse_count = padded - rows
    pairs = len(jobs) * rows * rows
    return pl.pallas_call(
        functools.partial(mass_kernel, jobs, len(arrays), len(small), n_out, finish, is_own),
        out_shape=tuple(
            jax.ShapeDtypeStruct((lse_count, LANES), jnp.float32) for _ in range(n_out)
        ),
        in_specs=[pl.BlockSpec(memory_space=pl.ANY)] * len(arrays)
        + [pl.BlockSpec(memory_space=pltpu.VMEM)] * len(small),
        out_specs=tuple(pl.BlockSpec(memory_space=pltpu.VMEM) for _ in range(n_out)),
        scratch_shapes=[
            pltpu.VMEM((len(jobs), rows, HD), jnp.bfloat16),
            pltpu.VMEM((len(jobs), rows, HD), jnp.bfloat16),
            pltpu.VMEM((len(jobs), lse_count, LANES), jnp.bfloat16),
            pltpu.VMEM((rows, LANES), jnp.float32),
            pltpu.VMEM((rows if is_own else 8, LANES), jnp.int32),
            pltpu.SemaphoreType.DMA((len(jobs), 3)),
        ],
        compiler_params=pltpu.CompilerParams(vmem_limit_bytes=VMEM_LIMIT),
        cost_estimate=pl.CostEstimate(
            flops=2 * pairs * HD, transcendentals=pairs, bytes_accessed=len(jobs) * 2**20
        ),
        name=name,
    )(*arrays, *small)


def job(x, x_steps, z, z_steps, out=0):
    return dict(x=x, x_steps=x_steps, z=z, z_steps=z_steps, out=out)


def finish_middle(role, results, small):
    middle, last = results
    return [middle, last, middle + small[0]]


def finish_last(role, results, small):
    own_a, own_b, first, middle, last_a = small
    zero = jnp.zeros_like(first)
    back = results[0] + last_a + jnp.where(role == 0, middle, zero)
    local = own_a + own_b + jnp.where(role == 0, first, zero)
    return [back, local]


def move(value, mesh_shape, steps_of_role):
    shards, heads = mesh_shape
    pairs = []
    for shard in range(shards):
        for head in range(heads):
            steps = steps_of_role[head % 2]
            if steps != 0 and 0 <= shard + steps < shards:
                pairs.append((shard * heads + head, (shard + steps) * heads + head))
    return lax.ppermute(value, ("ctx", "head"), pairs)


def after(value, *done):
    return lax.optimization_barrier((value, *done))[0]


def on_device(mesh_shape, key_rows, query_rows, row_lse, query_offsets):
    rows = query_rows.shape[0]
    out, back = (-1, 1), (1, -1)
    xa0, xb0, za0, zb0 = prepare(key_rows, query_rows, row_lse)
    offsets = query_offsets.reshape(rows // LANES, LANES)
    xa1 = move(xa0, mesh_shape, out)
    xb1 = move(after(xb0, xa0), mesh_shape, out)
    za1 = move(za0, mesh_shape, back)
    (own_a,) = mass_call("own_a", [xa0, za0], [job(0, 0, 1, 0)], (offsets,), is_own=True)
    xa1 = after(xa1, own_a)
    xa2 = move(xa1, mesh_shape, out)
    (own_b,) = mass_call(
        "own_b", [after(xb0, xa1), zb0], [job(0, 0, 1, 0)], (offsets,), is_own=True
    )
    xb1 = after(xb1, own_b)
    xb2 = move(xb1, mesh_shape, out)
    zb1 = move(after(zb0, own_b), mesh_shape, back)
    (first,) = mass_call(
        "first", [after(xa1, za1), za0, xb1, zb0], [job(0, 1, 1, 0), job(2, 1, 3, 0)]
    )
    middle, last_a, send = mass_call(
        "middle",
        [xa2, xa1, za1, xb1, zb1],
        [job(0, 2, 2, 1, out=1), job(1, 1, 2, 1), job(3, 1, 4, 1)],
        (first,),
        n_out=3,
        finish=finish_middle,
    )
    near = move(send, mesh_shape, (0, -1))
    far, local = mass_call(
        "last",
        [xb2, zb1],
        [job(0, 2, 1, 1)],
        (own_a, own_b, first, middle, last_a),
        n_out=2,
        finish=finish_last,
    )
    local = local + near + move(far, mesh_shape, (-1, -2))
    spread = lax.all_to_all(local, "head", 0, 0, tiled=True)
    return jnp.sum(spread, axis=0)


def solution(mesh):
    mesh_shape = (mesh.shape["ctx"], mesh.shape["head"])
    in_specs = (P("ctx", "head"), P("ctx", "head"), P("head", "ctx"), P("ctx"))
    out_specs = P(("ctx", "head"))
    return jax.shard_map(
        functools.partial(on_device, mesh_shape),
        mesh=mesh,
        in_specs=in_specs,
        out_specs=out_specs,
        check_vma=False,
    )
```

```python
import functools
import math

import jax
import jax.numpy as jnp
from jax import lax
from jax.experimental import pallas as pl
from jax.experimental.pallas import tpu as pltpu
from jax.sharding import PartitionSpec as P

HD = 128
LANES = 128
LOG2E = math.log2(math.e)
SCORE_SCALE = LOG2E / math.sqrt(HD)
DEAD = 1e30
STEP = 2.0**20
Q_TILE = 256
CONTRACT_LAST = (((1,), (1,)), ((), ()))
VMEM_LIMIT = 40 * 2**20


def role_of_device():
    return lax.rem(lax.axis_index("head"), 2)


def prepare_kernel(q_ref, k_ref, lse_ref, xa_ref, xb_ref, za_ref, zb_ref, wide, lse_rows, sems):
    rows = q_ref.shape[0]
    lse_count = rows // LANES
    role = role_of_device()

    def arrange(moving, fixed):
        lse_in = pltpu.make_async_copy(lse_ref, wide, sems.at[8])
        lse_in.start()
        copies = [
            pltpu.make_async_copy(moving.at[:, :HD], xa_ref.at[:rows], sems.at[0]),
            pltpu.make_async_copy(moving.at[:, HD:], xb_ref.at[:rows], sems.at[1]),
            pltpu.make_async_copy(fixed.at[:, :HD], za_ref.at[:rows], sems.at[2]),
            pltpu.make_async_copy(fixed.at[:, HD:], zb_ref.at[:rows], sems.at[3]),
        ]
        for copy in copies:
            copy.start()
        lse_in.wait()
        lse = wide[...].astype(jnp.float32)
        for head in range(2):
            pieces = [
                lse[head : head + 1, part * LANES : (part + 1) * LANES]
                for part in range(lse_count)
            ]
            lse_rows[head] = jnp.concatenate(pieces, axis=0).astype(jnp.bfloat16)
        for number, (ref, head) in enumerate(
            [(xa_ref, 0), (xb_ref, 1), (za_ref, 0), (zb_ref, 1)]
        ):
            copies.append(
                pltpu.make_async_copy(lse_rows.at[head], ref.at[rows:], sems.at[4 + number])
            )
            copies[-1].start()
        for copy in copies:
            copy.wait()

    pl.when(role == 0)(lambda: arrange(q_ref, k_ref))
    pl.when(role == 1)(lambda: arrange(k_ref, q_ref))


def prepare(key_rows, query_rows, row_lse):
    rows = query_rows.shape[0]
    lse_count = rows // LANES
    half = jax.ShapeDtypeStruct((rows + lse_count, HD), jnp.bfloat16)
    return pl.pallas_call(
        prepare_kernel,
        out_shape=(half,) * 4,
        in_specs=[
            pl.BlockSpec(memory_space=pltpu.HBM),
            pl.BlockSpec(memory_space=pltpu.HBM),
            pl.BlockSpec(memory_space=pltpu.HBM),
        ],
        out_specs=(pl.BlockSpec(memory_space=pl.ANY),) * 4,
        scratch_shapes=[
            pltpu.VMEM(row_lse.shape, jnp.bfloat16),
            pltpu.VMEM((2, lse_count, LANES), jnp.bfloat16),
            pltpu.SemaphoreType.DMA((9,)),
        ],
        compiler_params=pltpu.CompilerParams(vmem_limit_bytes=VMEM_LIMIT),
        name="prepare",
    )(
        pltpu.with_memory_space_constraint(query_rows, pltpu.HBM),
        pltpu.with_memory_space_constraint(key_rows, pltpu.HBM),
        pltpu.with_memory_space_constraint(row_lse, pltpu.HBM),
    )


def add_pair(q_buf, k_buf, lse_buf, offsets, key_steps, acc, is_first, is_live):
    lse = lse_buf[...].astype(jnp.float32) * LOG2E
    lse = jnp.where(is_live, lse, DEAD)
    parts = Q_TILE // LANES
    for tile in range(q_buf.shape[0] // Q_TILE):
        scores = lax.dot_general(
            k_buf[...],
            q_buf[tile * Q_TILE : (tile + 1) * Q_TILE, :],
            CONTRACT_LAST,
            preferred_element_type=jnp.float32,
        )
        total = None
        for part in range(parts):
            row = tile * parts + part
            exponent = (
                scores[:, part * LANES : (part + 1) * LANES] * SCORE_SCALE - lse[row : row + 1, :]
            )
            if offsets is not None:
                ceiling = offsets[row : row + 1, :] - key_steps[...]
                exponent = jnp.minimum(exponent, ceiling)
            weights = jnp.exp2(exponent)
            total = weights if total is None else total + weights
        if is_first and tile == 0:
            acc[...] = total
        else:
            acc[...] += total


def turned_mass(acc, count):
    parts = []
    for part in range(count):
        turned = acc[part * LANES : (part + 1) * LANES, :].T
        parts.append(jnp.sum(turned, axis=0, keepdims=True))
    return jnp.concatenate(parts, axis=0)


def mass_kernel(jobs, n_arrays, n_small, finish, is_own, *refs):
    arrays = refs[:n_arrays]
    small = refs[n_arrays : n_arrays + n_small]
    outs = refs[n_arrays + n_small : n_arrays + n_small + 1]
    q_buf, k_buf, lse_buf, acc, key_steps, sems = refs[n_arrays + n_small + 1 :]
    rows = q_buf.shape[1]
    lse_count = lse_buf.shape[1]
    role = role_of_device()
    shard = lax.axis_index("ctx")
    shards = lax.axis_size("ctx")

    def copies_of(number, chosen):
        query, key, _ = jobs[number][chosen]
        return [
            pltpu.make_async_copy(arrays[key].at[:rows], k_buf.at[number], sems.at[number, 0]),
            pltpu.make_async_copy(arrays[query].at[:rows], q_buf.at[number], sems.at[number, 1]),
            pltpu.make_async_copy(arrays[query].at[rows:], lse_buf.at[number], sems.at[number, 2]),
        ]

    def start_all(chosen):
        for number in range(len(jobs)):
            for copy in copies_of(number, chosen):
                copy.start()

    pl.when(role == 0)(lambda: start_all(0))
    pl.when(role == 1)(lambda: start_all(1))
    if is_own:
        first_rows = lax.broadcasted_iota(jnp.int32, (64, LANES), 0).astype(jnp.float32) * STEP

        def fill(number, carry):
            start = pl.multiple_of(number * 64, 64)
            key_steps[pl.ds(start, 64), :] = first_rows + start.astype(jnp.float32) * STEP
            return carry

        lax.fori_loop(0, rows // 64, fill, 0)
    for number, job in enumerate(jobs):
        for copy in copies_of(number, 0):
            copy.wait()
        add_pair(
            q_buf.at[number],
            k_buf.at[number],
            lse_buf.at[number],
            (small[0][...].astype(jnp.float32) + 0.5) * STEP if is_own else None,
            key_steps,
            acc,
            number == 0,
            shard + jnp.where(role == 0, job[0][2], job[1][2]) < shards,
        )
    mass = turned_mass(acc, lse_count)
    outs[0][...] = mass if finish is None else finish(role, mass, [ref[...] for ref in small])


def mass_call(name, arrays, jobs, small=(), finish=None, is_own=False):
    padded = arrays[0].shape[0]
    rows = padded * LANES // (LANES + 1)
    lse_count = padded - rows
    pairs = len(jobs) * rows * rows
    return pl.pallas_call(
        functools.partial(mass_kernel, jobs, len(arrays), len(small), finish, is_own),
        out_shape=jax.ShapeDtypeStruct((lse_count, LANES), jnp.float32),
        in_specs=[pl.BlockSpec(memory_space=pl.ANY)] * len(arrays)
        + [pl.BlockSpec(memory_space=pltpu.VMEM)] * len(small),
        out_specs=pl.BlockSpec(memory_space=pltpu.VMEM),
        scratch_shapes=[
            pltpu.VMEM((len(jobs), rows, HD), jnp.bfloat16),
            pltpu.VMEM((len(jobs), rows, HD), jnp.bfloat16),
            pltpu.VMEM((len(jobs), lse_count, LANES), jnp.bfloat16),
            pltpu.VMEM((rows, LANES), jnp.float32),
            pltpu.VMEM((rows if is_own else 8, LANES), jnp.float32),
            pltpu.SemaphoreType.DMA((len(jobs), 3)),
        ],
        compiler_params=pltpu.CompilerParams(vmem_limit_bytes=VMEM_LIMIT),
        cost_estimate=pl.CostEstimate(
            flops=2 * pairs * HD, transcendentals=pairs, bytes_accessed=len(jobs) * 2**20
        ),
        name=name,
    )(*arrays, *small)


def job(core_0, core_1):
    return (core_0, core_1)


def finish_last(role, mass, small):
    last_a, middle_a, middle_b = small
    return mass + last_a + jnp.where(role == 1, middle_a + middle_b, 0.0)


def finish_first(role, mass, small):
    own_a, own_b, middle_a, middle_b, first_a = small
    return mass + own_a + own_b + first_a + jnp.where(role == 0, middle_a + middle_b, 0.0)


def move(value, mesh_shape, steps_of_role):
    shards, heads = mesh_shape
    pairs = []
    for shard in range(shards):
        for head in range(heads):
            steps = steps_of_role[head % 2]
            if steps != 0 and 0 <= shard + steps < shards:
                pairs.append((shard * heads + head, (shard + steps) * heads + head))
    return lax.ppermute(value, ("ctx", "head"), pairs)


def after(value, *done):
    return lax.optimization_barrier((value, *done))[0]


def on_device(mesh_shape, key_rows, query_rows, row_lse, query_offsets):
    rows = query_rows.shape[0]
    out, back = (-1, 1), (1, -1)
    xa0, xb0, za0, zb0 = prepare(key_rows, query_rows, row_lse)
    offsets = query_offsets.reshape(rows // LANES, LANES)
    own = [job((0, 1, 0), (1, 0, 0))]
    middle = [job((0, 1, 2), (1, 0, 0))]
    last = [job((0, 1, 2), (1, 0, 1))]
    first = [job((0, 1, 1), (2, 3, 1))]

    xa1 = move(xa0, mesh_shape, out)
    xb1 = move(xb0, mesh_shape, out)
    za1 = move(za0, mesh_shape, back)
    own_a = mass_call("own_a", [xa0, za0], own, (offsets,), is_own=True)
    xa1 = after(xa1, own_a)
    xa2 = move(xa1, mesh_shape, out)
    own_b = mass_call("own_b", [after(xb0, xa1), zb0], own, (offsets,), is_own=True)
    xb1 = after(xb1, own_b)
    xb2 = move(xb1, mesh_shape, out)
    zb1 = move(after(zb0, xb1), mesh_shape, back)
    first_a = mass_call("first_a", [after(xa1, xb1), za0, za1, xa0], first)
    middle_a = mass_call("middle_a", [after(xa2, first_a), za0], middle)
    last_a = mass_call("last_a", [after(xa2, middle_a), za1], last)
    middle_b = mass_call("middle_b", [xb2, after(zb0, last_a)], middle)
    far = mass_call(
        "last_b",
        [xb2, after(zb1, middle_b)],
        last,
        (last_a, middle_a, middle_b),
        finish=finish_last,
    )
    local = mass_call(
        "first_b",
        [after(xb1, far), zb0, zb1, xb0],
        first,
        (own_a, own_b, middle_a, middle_b, first_a),
        finish=finish_first,
    )
    local = local + move(far, mesh_shape, (-1, -2))
    spread = lax.all_to_all(local, "head", 0, 0, tiled=True)
    return jnp.sum(spread, axis=0)


def solution(mesh):
    mesh_shape = (mesh.shape["ctx"], mesh.shape["head"])
    in_specs = (P("ctx", "head"), P("ctx", "head"), P("head", "ctx"), P("ctx"))
    out_specs = P(("ctx", "head"))
    return jax.shard_map(
        functools.partial(on_device, mesh_shape),
        mesh=mesh,
        in_specs=in_specs,
        out_specs=out_specs,
        check_vma=False,
    )
```

```python
import functools
import math

import jax
import jax.numpy as jnp
from jax import lax
from jax.experimental import pallas as pl
from jax.experimental.pallas import tpu as pltpu
from jax.sharding import PartitionSpec as P

HD = 128
LANES = 128
LOG2E = math.log2(math.e)
SCORE_SCALE = LOG2E / math.sqrt(HD)
DEAD = 1e30
STEP = 2.0**20
Q_TILE = 256
CONTRACT_LAST = (((1,), (1,)), ((), ()))
VMEM_LIMIT = 40 * 2**20


def role_of_device():
    return lax.rem(lax.axis_index("head"), 2)


def prepare_kernel(q_ref, k_ref, lse_ref, xa_ref, xb_ref, za_ref, zb_ref, wide, lse_rows, sems):
    rows = q_ref.shape[0]
    lse_count = rows // LANES
    role = role_of_device()

    def arrange(moving, fixed):
        lse_in = pltpu.make_async_copy(lse_ref, wide, sems.at[8])
        lse_in.start()
        copies = [
            pltpu.make_async_copy(moving.at[:, :HD], xa_ref.at[:rows], sems.at[0]),
            pltpu.make_async_copy(moving.at[:, HD:], xb_ref.at[:rows], sems.at[1]),
            pltpu.make_async_copy(fixed.at[:, :HD], za_ref.at[:rows], sems.at[2]),
            pltpu.make_async_copy(fixed.at[:, HD:], zb_ref.at[:rows], sems.at[3]),
        ]
        for copy in copies:
            copy.start()
        lse_in.wait()
        lse = wide[...].astype(jnp.float32)
        for head in range(2):
            pieces = [
                lse[head : head + 1, part * LANES : (part + 1) * LANES]
                for part in range(lse_count)
            ]
            lse_rows[head] = jnp.concatenate(pieces, axis=0).astype(jnp.bfloat16)
        for number, (ref, head) in enumerate(
            [(xa_ref, 0), (xb_ref, 1), (za_ref, 0), (zb_ref, 1)]
        ):
            copies.append(
                pltpu.make_async_copy(lse_rows.at[head], ref.at[rows:], sems.at[4 + number])
            )
            copies[-1].start()
        for copy in copies:
            copy.wait()

    pl.when(role == 0)(lambda: arrange(q_ref, k_ref))
    pl.when(role == 1)(lambda: arrange(k_ref, q_ref))


def prepare(key_rows, query_rows, row_lse):
    rows = query_rows.shape[0]
    lse_count = rows // LANES
    half = jax.ShapeDtypeStruct((rows + lse_count, HD), jnp.bfloat16)
    return pl.pallas_call(
        prepare_kernel,
        out_shape=(half,) * 4,
        in_specs=[
            pl.BlockSpec(memory_space=pltpu.HBM),
            pl.BlockSpec(memory_space=pltpu.HBM),
            pl.BlockSpec(memory_space=pltpu.HBM),
        ],
        out_specs=(pl.BlockSpec(memory_space=pl.ANY),) * 4,
        scratch_shapes=[
            pltpu.VMEM(row_lse.shape, jnp.bfloat16),
            pltpu.VMEM((2, lse_count, LANES), jnp.bfloat16),
            pltpu.SemaphoreType.DMA((9,)),
        ],
        compiler_params=pltpu.CompilerParams(vmem_limit_bytes=VMEM_LIMIT),
        name="prepare",
    )(
        pltpu.with_memory_space_constraint(query_rows, pltpu.HBM),
        pltpu.with_memory_space_constraint(key_rows, pltpu.HBM),
        pltpu.with_memory_space_constraint(row_lse, pltpu.HBM),
    )


def add_pair(q_buf, k_buf, lse_buf, offsets, key_steps, acc, is_first, is_live):
    lse = lse_buf[...].astype(jnp.float32) * LOG2E
    lse = jnp.where(is_live, lse, DEAD)
    parts = Q_TILE // LANES
    for tile in range(q_buf.shape[0] // Q_TILE):
        scores = lax.dot_general(
            k_buf[...],
            q_buf[tile * Q_TILE : (tile + 1) * Q_TILE, :],
            CONTRACT_LAST,
            preferred_element_type=jnp.float32,
        )
        total = None
        for part in range(parts):
            row = tile * parts + part
            exponent = (
                scores[:, part * LANES : (part + 1) * LANES] * SCORE_SCALE - lse[row : row + 1, :]
            )
            if offsets is not None:
                ceiling = offsets[row : row + 1, :] - key_steps[...]
                exponent = jnp.minimum(exponent, ceiling)
            weights = jnp.exp2(exponent)
            total = weights if total is None else total + weights
        if is_first and tile == 0:
            acc[...] = total
        else:
            acc[...] += total


def turned_mass(acc, count):
    parts = []
    for part in range(count):
        turned = acc[part * LANES : (part + 1) * LANES, :].T
        parts.append(jnp.sum(turned, axis=0, keepdims=True))
    return jnp.concatenate(parts, axis=0)


def mass_kernel(jobs, n_arrays, n_small, finish, is_own, *refs):
    arrays = refs[:n_arrays]
    small = refs[n_arrays : n_arrays + n_small]
    outs = refs[n_arrays + n_small : n_arrays + n_small + 1]
    q_buf, k_buf, lse_buf, acc, key_steps, sems = refs[n_arrays + n_small + 1 :]
    rows = q_buf.shape[1]
    lse_count = lse_buf.shape[1]
    role = role_of_device()
    shard = lax.axis_index("ctx")
    shards = lax.axis_size("ctx")

    upper = shard >= shards // 2

    def copies_of(number, chosen):
        query, key, _ = jobs[number][chosen]
        return [
            pltpu.make_async_copy(arrays[key].at[:rows], k_buf.at[number], sems.at[number, 0]),
            pltpu.make_async_copy(arrays[query].at[:rows], q_buf.at[number], sems.at[number, 1]),
            pltpu.make_async_copy(arrays[query].at[rows:], lse_buf.at[number], sems.at[number, 2]),
        ]

    def start_job(number, chosen):
        for copy in copies_of(number, chosen):
            copy.start()

    for number, (_, _, gate) in enumerate(jobs):
        wanted = True if gate is None else gate(role, upper)
        for chosen in range(2):
            if jobs[number][chosen] is not None:
                pl.when((role == chosen) & wanted)(functools.partial(start_job, number, chosen))
    if is_own:
        first_rows = lax.broadcasted_iota(jnp.int32, (64, LANES), 0).astype(jnp.float32) * STEP

        def fill(number, carry):
            start = pl.multiple_of(number * 64, 64)
            key_steps[pl.ds(start, 64), :] = first_rows + start.astype(jnp.float32) * STEP
            return carry

        lax.fori_loop(0, rows // 64, fill, 0)
    def run(number):
        chosen = 0 if jobs[number][0] is not None else 1
        for copy in copies_of(number, chosen):
            copy.wait()
        steps = [0 if entry is None else entry[2] for entry in jobs[number][:2]]
        add_pair(
            q_buf.at[number],
            k_buf.at[number],
            lse_buf.at[number],
            (small[0][...].astype(jnp.float32) + 0.5) * STEP if is_own else None,
            key_steps,
            acc,
            number == 0,
            shard + jnp.where(role == 0, steps[0], steps[1]) < shards,
        )

    for number, (_, _, gate) in enumerate(jobs):
        if gate is None:
            run(number)
            continue
        wanted = gate(role, upper)
        if number == 0:

            @pl.when(jnp.logical_not(wanted))
            def _():
                acc[...] = jnp.zeros_like(acc)

        pl.when(wanted)(functools.partial(run, number))
    mass = turned_mass(acc, lse_count)
    outs[0][...] = mass if finish is None else finish(role, mass, [ref[...] for ref in small])


def mass_call(name, arrays, jobs, small=(), finish=None, is_own=False):
    padded = arrays[0].shape[0]
    rows = padded * LANES // (LANES + 1)
    lse_count = padded - rows
    pairs = len(jobs) * rows * rows
    return pl.pallas_call(
        functools.partial(mass_kernel, jobs, len(arrays), len(small), finish, is_own),
        out_shape=jax.ShapeDtypeStruct((lse_count, LANES), jnp.float32),
        in_specs=[pl.BlockSpec(memory_space=pl.ANY)] * len(arrays)
        + [pl.BlockSpec(memory_space=pltpu.VMEM)] * len(small),
        out_specs=pl.BlockSpec(memory_space=pltpu.VMEM),
        scratch_shapes=[
            pltpu.VMEM((len(jobs), rows, HD), jnp.bfloat16),
            pltpu.VMEM((len(jobs), rows, HD), jnp.bfloat16),
            pltpu.VMEM((len(jobs), lse_count, LANES), jnp.bfloat16),
            pltpu.VMEM((rows, LANES), jnp.float32),
            pltpu.VMEM((rows if is_own else 8, LANES), jnp.float32),
            pltpu.SemaphoreType.DMA((len(jobs), 3)),
        ],
        compiler_params=pltpu.CompilerParams(vmem_limit_bytes=VMEM_LIMIT),
        cost_estimate=pl.CostEstimate(
            flops=2 * pairs * HD, transcendentals=pairs, bytes_accessed=len(jobs) * 2**20
        ),
        name=name,
    )(*arrays, *small)


def job(core_0, core_1, gate=None):
    return (core_0, core_1, gate)


def runs_early(role, upper):
    return (role == 1) | upper


def runs_late(role, upper):
    return (role == 0) & jnp.logical_not(upper)


def finish_far(role, mass, small):
    last_a, middle_a, middle_b = small
    return mass + last_a + jnp.where(role == 1, middle_a + middle_b, 0.0)


def finish_near(role, mass, small):
    own_a, own_b, first_a, middle_a, middle_b = small
    return mass + own_a + own_b + first_a + jnp.where(role == 0, middle_a + middle_b, 0.0)


def move(value, mesh_shape, steps_of_role):
    shards, heads = mesh_shape
    pairs = []
    for shard in range(shards):
        for head in range(heads):
            steps = steps_of_role[head % 2]
            if steps != 0 and 0 <= shard + steps < shards:
                pairs.append((shard * heads + head, (shard + steps) * heads + head))
    return lax.ppermute(value, ("ctx", "head"), pairs)


def after(value, *done):
    return lax.optimization_barrier((value, *done))[0]


def on_device(mesh_shape, key_rows, query_rows, row_lse, query_offsets):
    rows = query_rows.shape[0]
    out, back = (-1, 1), (1, -1)
    xa0, xb0, za0, zb0 = prepare(key_rows, query_rows, row_lse)
    offsets = query_offsets.reshape(rows // LANES, LANES)
    own = [job((0, 1, 0), (1, 0, 0))]
    middle = [job((0, 1, 2), (1, 0, 0))]
    last = [job((0, 1, 2), (1, 0, 1))]
    middle_early = [job((0, 1, 2), (1, 0, 0), runs_early)]
    first = [job((0, 1, 1), (2, 3, 1))]
    near_jobs = [job((0, 1, 1), (2, 3, 1)), job((4, 1, 2), None, runs_late)]

    xa1 = move(xa0, mesh_shape, out)
    xb1 = move(xb0, mesh_shape, out)
    za1 = move(za0, mesh_shape, back)
    own_a = mass_call("own_a", [xa0, za0], own, (offsets,), is_own=True)
    xa1 = after(xa1, own_a)
    xa2 = move(xa1, mesh_shape, out)
    own_b = mass_call("own_b", [after(xb0, xa1), zb0], own, (offsets,), is_own=True)
    xb1 = after(xb1, own_b)
    xb2 = move(xb1, mesh_shape, out)
    zb1 = move(after(zb0, xb1, za1), mesh_shape, back)
    middle_a = mass_call("middle_a", [after(xa2, xb1, za1), za0], middle)
    last_a = mass_call("last_a", [after(xa2, middle_a), za1], last)
    first_a = mass_call("first_a", [after(xa1, last_a), za0, za1, xa0], first)
    middle_b = mass_call("middle_b", [xb2, after(zb0, first_a)], middle_early)
    far = mass_call(
        "last_b",
        [xb2, after(zb1, middle_b)],
        last,
        (last_a, middle_a, middle_b),
        finish=finish_far,
    )
    local = mass_call(
        "near",
        [after(xb1, far), zb0, zb1, xb0, xb2],
        near_jobs,
        (own_a, own_b, first_a, middle_a, middle_b),
        finish=finish_near,
    )
    local = local + move(far, mesh_shape, (-1, -2))
    spread = lax.all_to_all(local, "head", 0, 0, tiled=True)
    return jnp.sum(spread, axis=0)


def solution(mesh):
    mesh_shape = (mesh.shape["ctx"], mesh.shape["head"])
    in_specs = (P("ctx", "head"), P("ctx", "head"), P("head", "ctx"), P("ctx"))
    out_specs = P(("ctx", "head"))
    return jax.shard_map(
        functools.partial(on_device, mesh_shape),
        mesh=mesh,
        in_specs=in_specs,
        out_specs=out_specs,
        check_vma=False,
    )
```

```python
import functools
import math

import jax
import jax.numpy as jnp
from jax import lax
from jax.experimental import pallas as pl
from jax.experimental.pallas import tpu as pltpu
from jax.sharding import PartitionSpec as P

HD = 128
LANES = 128
LOG2E = math.log2(math.e)
SCORE_SCALE = LOG2E / math.sqrt(HD)
DEAD = 1e30
STEP = 2.0**20
Q_TILE = 256
CONTRACT_LAST = (((1,), (1,)), ((), ()))
VMEM_LIMIT = 40 * 2**20


def role_of_device():
    return lax.rem(lax.axis_index("head"), 2)


def prepare_kernel(q_ref, k_ref, lse_ref, xa_ref, xb_ref, za_ref, zb_ref, wide, lse_rows, sems):
    rows = q_ref.shape[0]
    lse_count = rows // LANES
    role = role_of_device()

    def arrange(moving, fixed):
        lse_in = pltpu.make_async_copy(lse_ref, wide, sems.at[8])
        lse_in.start()
        copies = [
            pltpu.make_async_copy(moving.at[:, :HD], xa_ref.at[:rows], sems.at[0]),
            pltpu.make_async_copy(moving.at[:, HD:], xb_ref.at[:rows], sems.at[1]),
            pltpu.make_async_copy(fixed.at[:, :HD], za_ref.at[:rows], sems.at[2]),
            pltpu.make_async_copy(fixed.at[:, HD:], zb_ref.at[:rows], sems.at[3]),
        ]
        for copy in copies:
            copy.start()
        lse_in.wait()
        lse = wide[...].astype(jnp.float32)
        for head in range(2):
            pieces = [
                lse[head : head + 1, part * LANES : (part + 1) * LANES]
                for part in range(lse_count)
            ]
            lse_rows[head] = jnp.concatenate(pieces, axis=0).astype(jnp.bfloat16)
        for number, (ref, head) in enumerate(
            [(xa_ref, 0), (xb_ref, 1), (za_ref, 0), (zb_ref, 1)]
        ):
            copies.append(
                pltpu.make_async_copy(lse_rows.at[head], ref.at[rows:], sems.at[4 + number])
            )
            copies[-1].start()
        for copy in copies:
            copy.wait()

    pl.when(role == 0)(lambda: arrange(q_ref, k_ref))
    pl.when(role == 1)(lambda: arrange(k_ref, q_ref))


def prepare(key_rows, query_rows, row_lse):
    rows = query_rows.shape[0]
    lse_count = rows // LANES
    half = jax.ShapeDtypeStruct((rows + lse_count, HD), jnp.bfloat16)
    return pl.pallas_call(
        prepare_kernel,
        out_shape=(half,) * 4,
        in_specs=[
            pl.BlockSpec(memory_space=pltpu.HBM),
            pl.BlockSpec(memory_space=pltpu.HBM),
            pl.BlockSpec(memory_space=pltpu.HBM),
        ],
        out_specs=(pl.BlockSpec(memory_space=pl.ANY),) * 4,
        scratch_shapes=[
            pltpu.VMEM(row_lse.shape, jnp.bfloat16),
            pltpu.VMEM((2, lse_count, LANES), jnp.bfloat16),
            pltpu.SemaphoreType.DMA((9,)),
        ],
        compiler_params=pltpu.CompilerParams(vmem_limit_bytes=VMEM_LIMIT),
        name="prepare",
    )(
        pltpu.with_memory_space_constraint(query_rows, pltpu.HBM),
        pltpu.with_memory_space_constraint(key_rows, pltpu.HBM),
        pltpu.with_memory_space_constraint(row_lse, pltpu.HBM),
    )


def add_pair(q_buf, k_buf, lse_buf, offsets, key_steps, acc, is_first, is_live):
    lse = lse_buf[...].astype(jnp.float32) * LOG2E
    lse = jnp.where(is_live, lse, DEAD)
    parts = Q_TILE // LANES
    for tile in range(q_buf.shape[0] // Q_TILE):
        scores = lax.dot_general(
            k_buf[...],
            q_buf[tile * Q_TILE : (tile + 1) * Q_TILE, :],
            CONTRACT_LAST,
            preferred_element_type=jnp.float32,
        )
        total = None
        for part in range(parts):
            row = tile * parts + part
            exponent = (
                scores[:, part * LANES : (part + 1) * LANES] * SCORE_SCALE - lse[row : row + 1, :]
            )
            if offsets is not None:
                ceiling = offsets[row : row + 1, :] - key_steps[...]
                exponent = jnp.minimum(exponent, ceiling)
            weights = jnp.exp2(exponent)
            total = weights if total is None else total + weights
        if is_first and tile == 0:
            acc[...] = total
        else:
            acc[...] += total


def turned_mass(acc, count):
    parts = []
    for part in range(count):
        turned = acc[part * LANES : (part + 1) * LANES, :].T
        parts.append(jnp.sum(turned, axis=0, keepdims=True))
    return jnp.concatenate(parts, axis=0)


def mass_kernel(jobs, n_arrays, n_small, finish, is_own, *refs):
    arrays = refs[:n_arrays]
    small = refs[n_arrays : n_arrays + n_small]
    outs = refs[n_arrays + n_small : n_arrays + n_small + 1]
    q_buf, k_buf, lse_buf, acc, key_steps, sems = refs[n_arrays + n_small + 1 :]
    rows = q_buf.shape[1]
    lse_count = lse_buf.shape[1]
    role = role_of_device()
    shard = lax.axis_index("ctx")
    shards = lax.axis_size("ctx")

    upper = shard >= shards // 2

    def copies_of(number, chosen, relayed=False):
        query, key, _ = jobs[number][chosen]
        if isinstance(query, tuple):
            query = query[1 if relayed else 0]
        return [
            pltpu.make_async_copy(arrays[key].at[:rows], k_buf.at[number], sems.at[number, 0]),
            pltpu.make_async_copy(arrays[query].at[:rows], q_buf.at[number], sems.at[number, 1]),
            pltpu.make_async_copy(arrays[query].at[rows:], lse_buf.at[number], sems.at[number, 2]),
        ]

    def start_job(number, chosen, relayed):
        for copy in copies_of(number, chosen, relayed):
            copy.start()

    at_target = shard == shards // 2 - 1
    for number, (_, _, gate) in enumerate(jobs):
        wanted = True if gate is None else gate(role, upper)
        for chosen in range(2):
            entry = jobs[number][chosen]
            if entry is None:
                continue
            here = (role == chosen) & wanted
            if isinstance(entry[0], tuple):
                pl.when(here & at_target)(functools.partial(start_job, number, chosen, True))
                here = here & jnp.logical_not(at_target)
            pl.when(here)(functools.partial(start_job, number, chosen, False))
    if is_own:
        first_rows = lax.broadcasted_iota(jnp.int32, (64, LANES), 0).astype(jnp.float32) * STEP

        def fill(number, carry):
            start = pl.multiple_of(number * 64, 64)
            key_steps[pl.ds(start, 64), :] = first_rows + start.astype(jnp.float32) * STEP
            return carry

        lax.fori_loop(0, rows // 64, fill, 0)
    def run(number):
        chosen = 0 if jobs[number][0] is not None else 1
        for copy in copies_of(number, chosen):
            copy.wait()
        steps = [0 if entry is None else entry[2] for entry in jobs[number][:2]]
        add_pair(
            q_buf.at[number],
            k_buf.at[number],
            lse_buf.at[number],
            (small[0][...].astype(jnp.float32) + 0.5) * STEP if is_own else None,
            key_steps,
            acc,
            number == 0,
            shard + jnp.where(role == 0, steps[0], steps[1]) < shards,
        )

    for number, (_, _, gate) in enumerate(jobs):
        if gate is None:
            run(number)
            continue
        wanted = gate(role, upper)
        if number == 0:

            @pl.when(jnp.logical_not(wanted))
            def _():
                acc[...] = jnp.zeros_like(acc)

        pl.when(wanted)(functools.partial(run, number))
    mass = turned_mass(acc, lse_count)
    outs[0][...] = mass if finish is None else finish(role, mass, [ref[...] for ref in small])


def mass_call(name, arrays, jobs, small=(), finish=None, is_own=False):
    padded = arrays[0].shape[0]
    rows = padded * LANES // (LANES + 1)
    lse_count = padded - rows
    pairs = len(jobs) * rows * rows
    return pl.pallas_call(
        functools.partial(mass_kernel, jobs, len(arrays), len(small), finish, is_own),
        out_shape=jax.ShapeDtypeStruct((lse_count, LANES), jnp.float32),
        in_specs=[pl.BlockSpec(memory_space=pl.ANY)] * len(arrays)
        + [pl.BlockSpec(memory_space=pltpu.VMEM)] * len(small),
        out_specs=pl.BlockSpec(memory_space=pltpu.VMEM),
        scratch_shapes=[
            pltpu.VMEM((len(jobs), rows, HD), jnp.bfloat16),
            pltpu.VMEM((len(jobs), rows, HD), jnp.bfloat16),
            pltpu.VMEM((len(jobs), lse_count, LANES), jnp.bfloat16),
            pltpu.VMEM((rows, LANES), jnp.float32),
            pltpu.VMEM((rows if is_own else 8, LANES), jnp.float32),
            pltpu.SemaphoreType.DMA((len(jobs), 3)),
        ],
        compiler_params=pltpu.CompilerParams(vmem_limit_bytes=VMEM_LIMIT),
        cost_estimate=pl.CostEstimate(
            flops=2 * pairs * HD, transcendentals=pairs, bytes_accessed=len(jobs) * 2**20
        ),
        name=name,
    )(*arrays, *small)


def job(core_0, core_1, gate=None):
    return (core_0, core_1, gate)


def core_1(role, upper):
    return role == 1


def core_0(role, upper):
    return role == 0


def core_0_lower(role, upper):
    return (role == 0) & jnp.logical_not(upper)


def core_0_upper(role, upper):
    return (role == 0) & upper


def not_core_0_lower(role, upper):
    return (role == 1) | upper


def not_core_0_upper(role, upper):
    return (role == 1) | jnp.logical_not(upper)


def finish_far(role, mass, small):
    last_a, middle_a, middle_b = small
    return mass + last_a + jnp.where(role == 1, middle_a + middle_b, 0.0)


def finish_near(role, mass, small):
    own_a, own_b, first_a, middle_a, middle_b = small
    return mass + own_a + own_b + first_a + jnp.where(role == 0, middle_a + middle_b, 0.0)


def move(value, mesh_shape, steps_of_role):
    shards, heads = mesh_shape
    pairs = []
    for shard in range(shards):
        for head in range(heads):
            steps = steps_of_role[head % 2]
            if steps != 0 and 0 <= shard + steps < shards:
                pairs.append((shard * heads + head, (shard + steps) * heads + head))
    return lax.ppermute(value, ("ctx", "head"), pairs)


def move_around(value, mesh_shape):
    shards, heads = mesh_shape
    pairs = []
    for shard in range(shards):
        for head in range(heads):
            if head % 2 == 1 and shard == shards // 2:
                pairs.append((shard * heads + head, head - 1))
            elif head % 2 == 1 and shard > 0:
                pairs.append((shard * heads + head, (shard - 1) * heads + head))
    return lax.ppermute(value, ("ctx", "head"), pairs)


def move_on(value, mesh_shape):
    shards, heads = mesh_shape
    target = shards // 2 - 1
    pairs = [(head, target * heads + head + 1) for head in range(0, heads, 2)]
    return lax.ppermute(value, ("ctx", "head"), pairs)


def after(value, *done):
    return lax.optimization_barrier((value, *done))[0]


def on_device(mesh_shape, key_rows, query_rows, row_lse, query_offsets):
    rows = query_rows.shape[0]
    out, back = (-1, 1), (1, -1)
    xa0, xb0, za0, zb0 = prepare(key_rows, query_rows, row_lse)
    offsets = query_offsets.reshape(rows // LANES, LANES)
    own = [job((0, 1, 0), (1, 0, 0))]
    middle = [job((0, 1, 2), (1, 0, 0))]
    last_relayed = [job((0, 1, 2), ((2, 3), 0, 1))]
    last = [job((0, 1, 2), (1, 0, 1))]
    first_early = [job((0, 1, 1), ((2, 4), 3, 1), not_core_0_lower)]
    middle_early = [job(None, (1, 0, 0), core_1), job((2, 1, 1), None, core_0_upper)]
    near_jobs = [
        job((0, 1, 1), (2, 3, 1), not_core_0_upper),
        job((4, 1, 2), None, core_0),
        job((5, 6, 1), None, core_0_lower),
    ]

    xa1 = move(xa0, mesh_shape, out)
    xb1 = move(xb0, mesh_shape, out)
    za1_core_1 = move_around(za0, mesh_shape)
    za1_core_0 = move(za0, mesh_shape, (1, 0))
    own_a = mass_call("own_a", [xa0, za0], own, (offsets,), is_own=True)
    xa1 = after(xa1, own_a)
    xa2 = move(xa1, mesh_shape, out)
    xb1 = after(xb1, xa1)
    xb2 = move(xb1, mesh_shape, out)
    za1_core_1 = after(za1_core_1, xb1)
    za1_relayed = move_on(za1_core_1, mesh_shape)
    zb0 = after(zb0, xb1, za1_core_1)
    zb1 = move(zb0, mesh_shape, back)
    own_b = mass_call("own_b", [after(xb0, za1_core_0), zb0], own, (offsets,), is_own=True)
    middle_a = mass_call("middle_a", [after(xa2, own_b), za0], middle)
    last_a = mass_call(
        "last_a",
        [after(xa2, middle_a), za1_core_0, za1_core_1, za1_relayed],
        last_relayed,
    )
    first_a = mass_call(
        "first_a", [after(xa1, last_a), za0, za1_core_1, xa0, za1_relayed], first_early
    )
    middle_b = mass_call("middle_b", [xb2, after(zb0, first_a), xb1], middle_early)
    far = mass_call(
        "last_b",
        [xb2, after(zb1, middle_b)],
        last,
        (last_a, middle_a, middle_b),
        finish=finish_far,
    )
    local = mass_call(
        "near",
        [after(xb1, far), zb0, zb1, xb0, xb2, xa1, za0],
        near_jobs,
        (own_a, own_b, first_a, middle_a, middle_b),
        finish=finish_near,
    )
    local = local + move(far, mesh_shape, (-1, -2))
    spread = lax.all_to_all(local, "head", 0, 0, tiled=True)
    return jnp.sum(spread, axis=0)


def solution(mesh):
    mesh_shape = (mesh.shape["ctx"], mesh.shape["head"])
    in_specs = (P("ctx", "head"), P("ctx", "head"), P("head", "ctx"), P("ctx"))
    out_specs = P(("ctx", "head"))
    return jax.shard_map(
        functools.partial(on_device, mesh_shape),
        mesh=mesh,
        in_specs=in_specs,
        out_specs=out_specs,
        check_vma=False,
    )
```

```python
import functools
import math

import jax
import jax.numpy as jnp
from jax import lax
from jax.experimental import pallas as pl
from jax.experimental.pallas import tpu as pltpu
from jax.sharding import PartitionSpec as P

HD = 128
LANES = 128
LOG2E = math.log2(math.e)
SCORE_SCALE = LOG2E / math.sqrt(HD)
DEAD = 1e30
STEP = 2.0**20
Q_TILE = 256
CONTRACT_LAST = (((1,), (1,)), ((), ()))
VMEM_LIMIT = 40 * 2**20


def role_of_device():
    return lax.rem(lax.axis_index("head"), 2)


def prepare_kernel(q_ref, k_ref, lse_ref, xa_ref, xb_ref, za_ref, zb_ref, wide, lse_rows, sems):
    rows = q_ref.shape[0]
    lse_count = rows // LANES
    role = role_of_device()

    def arrange(moving, fixed):
        lse_in = pltpu.make_async_copy(lse_ref, wide, sems.at[8])
        lse_in.start()
        copies = [
            pltpu.make_async_copy(moving.at[:, :HD], xa_ref.at[:rows], sems.at[0]),
            pltpu.make_async_copy(moving.at[:, HD:], xb_ref.at[:rows], sems.at[1]),
            pltpu.make_async_copy(fixed.at[:, :HD], za_ref.at[:rows], sems.at[2]),
            pltpu.make_async_copy(fixed.at[:, HD:], zb_ref.at[:rows], sems.at[3]),
        ]
        for copy in copies:
            copy.start()
        lse_in.wait()
        lse = wide[...].astype(jnp.float32)
        for head in range(2):
            pieces = [
                lse[head : head + 1, part * LANES : (part + 1) * LANES]
                for part in range(lse_count)
            ]
            lse_rows[head] = jnp.concatenate(pieces, axis=0).astype(jnp.bfloat16)
        for number, (ref, head) in enumerate(
            [(xa_ref, 0), (xb_ref, 1), (za_ref, 0), (zb_ref, 1)]
        ):
            copies.append(
                pltpu.make_async_copy(lse_rows.at[head], ref.at[rows:], sems.at[4 + number])
            )
            copies[-1].start()
        for copy in copies:
            copy.wait()

    pl.when(role == 0)(lambda: arrange(q_ref, k_ref))
    pl.when(role == 1)(lambda: arrange(k_ref, q_ref))


def prepare(key_rows, query_rows, row_lse):
    rows = query_rows.shape[0]
    lse_count = rows // LANES
    half = jax.ShapeDtypeStruct((rows + lse_count, HD), jnp.bfloat16)
    return pl.pallas_call(
        prepare_kernel,
        out_shape=(half,) * 4,
        in_specs=[
            pl.BlockSpec(memory_space=pltpu.HBM),
            pl.BlockSpec(memory_space=pltpu.HBM),
            pl.BlockSpec(memory_space=pltpu.HBM),
        ],
        out_specs=(pl.BlockSpec(memory_space=pl.ANY),) * 4,
        scratch_shapes=[
            pltpu.VMEM(row_lse.shape, jnp.bfloat16),
            pltpu.VMEM((2, lse_count, LANES), jnp.bfloat16),
            pltpu.SemaphoreType.DMA((9,)),
        ],
        compiler_params=pltpu.CompilerParams(vmem_limit_bytes=VMEM_LIMIT),
        name="prepare",
    )(
        pltpu.with_memory_space_constraint(query_rows, pltpu.HBM),
        pltpu.with_memory_space_constraint(key_rows, pltpu.HBM),
        pltpu.with_memory_space_constraint(row_lse, pltpu.HBM),
    )


def add_pair(q_buf, k_buf, lse_buf, offsets, key_steps, acc, is_first, is_live):
    lse = lse_buf[...].astype(jnp.float32) * LOG2E
    lse = jnp.where(is_live, lse, DEAD)
    parts = Q_TILE // LANES
    for tile in range(q_buf.shape[0] // Q_TILE):
        scores = lax.dot_general(
            k_buf[...],
            q_buf[tile * Q_TILE : (tile + 1) * Q_TILE, :],
            CONTRACT_LAST,
            preferred_element_type=jnp.float32,
        )
        total = None
        for part in range(parts):
            row = tile * parts + part
            exponent = (
                scores[:, part * LANES : (part + 1) * LANES] * SCORE_SCALE - lse[row : row + 1, :]
            )
            if offsets is not None:
                ceiling = offsets[row : row + 1, :] - key_steps[...]
                exponent = jnp.minimum(exponent, ceiling)
            weights = jnp.exp2(exponent)
            total = weights if total is None else total + weights
        if is_first and tile == 0:
            acc[...] = total
        else:
            acc[...] += total


def turned_mass(acc, count):
    parts = []
    for part in range(count):
        turned = acc[part * LANES : (part + 1) * LANES, :].T
        parts.append(jnp.sum(turned, axis=0, keepdims=True))
    return jnp.concatenate(parts, axis=0)


def mass_kernel(jobs, n_arrays, n_small, finish, is_own, *refs):
    arrays = refs[:n_arrays]
    small = refs[n_arrays : n_arrays + n_small]
    outs = refs[n_arrays + n_small : n_arrays + n_small + 1]
    q_buf, k_buf, lse_buf, acc, key_steps, sems = refs[n_arrays + n_small + 1 :]
    rows = q_buf.shape[1]
    lse_count = lse_buf.shape[1]
    role = role_of_device()
    shard = lax.axis_index("ctx")
    shards = lax.axis_size("ctx")

    upper = shard >= shards // 2

    def copies_of(number, chosen, relayed=False):
        query, key, _ = jobs[number][chosen]
        if isinstance(query, tuple):
            query = query[1 if relayed else 0]
        return [
            pltpu.make_async_copy(arrays[key].at[:rows], k_buf.at[number], sems.at[number, 0]),
            pltpu.make_async_copy(arrays[query].at[:rows], q_buf.at[number], sems.at[number, 1]),
            pltpu.make_async_copy(arrays[query].at[rows:], lse_buf.at[number], sems.at[number, 2]),
        ]

    def start_job(number, chosen, relayed):
        for copy in copies_of(number, chosen, relayed):
            copy.start()

    at_target = shard == shards // 2 - 1
    for number, (_, _, gate) in enumerate(jobs):
        wanted = True if gate is None else gate(role, upper)
        for chosen in range(2):
            entry = jobs[number][chosen]
            if entry is None:
                continue
            here = (role == chosen) & wanted
            if isinstance(entry[0], tuple):
                pl.when(here & at_target)(functools.partial(start_job, number, chosen, True))
                here = here & jnp.logical_not(at_target)
            pl.when(here)(functools.partial(start_job, number, chosen, False))
    if is_own:
        first_rows = lax.broadcasted_iota(jnp.int32, (64, LANES), 0).astype(jnp.float32) * STEP

        def fill(number, carry):
            start = pl.multiple_of(number * 64, 64)
            key_steps[pl.ds(start, 64), :] = first_rows + start.astype(jnp.float32) * STEP
            return carry

        lax.fori_loop(0, rows // 64, fill, 0)
    def run(number):
        chosen = 0 if jobs[number][0] is not None else 1
        for copy in copies_of(number, chosen):
            copy.wait()
        steps = [0 if entry is None else entry[2] for entry in jobs[number][:2]]
        add_pair(
            q_buf.at[number],
            k_buf.at[number],
            lse_buf.at[number],
            (small[0][...].astype(jnp.float32) + 0.5) * STEP if is_own else None,
            key_steps,
            acc,
            number == 0,
            shard + jnp.where(role == 0, steps[0], steps[1]) < shards,
        )

    for number, (_, _, gate) in enumerate(jobs):
        if gate is None:
            run(number)
            continue
        wanted = gate(role, upper)
        if number == 0:

            @pl.when(jnp.logical_not(wanted))
            def _():
                acc[...] = jnp.zeros_like(acc)

        pl.when(wanted)(functools.partial(run, number))
    mass = turned_mass(acc, lse_count)
    outs[0][...] = mass if finish is None else finish(role, mass, [ref[...] for ref in small])


def mass_call(name, arrays, jobs, small=(), finish=None, is_own=False):
    padded = arrays[0].shape[0]
    rows = padded * LANES // (LANES + 1)
    lse_count = padded - rows
    pairs = len(jobs) * rows * rows
    return pl.pallas_call(
        functools.partial(mass_kernel, jobs, len(arrays), len(small), finish, is_own),
        out_shape=jax.ShapeDtypeStruct((lse_count, LANES), jnp.float32),
        in_specs=[pl.BlockSpec(memory_space=pl.ANY)] * len(arrays)
        + [pl.BlockSpec(memory_space=pltpu.VMEM)] * len(small),
        out_specs=pl.BlockSpec(memory_space=pltpu.VMEM),
        scratch_shapes=[
            pltpu.VMEM((len(jobs), rows, HD), jnp.bfloat16),
            pltpu.VMEM((len(jobs), rows, HD), jnp.bfloat16),
            pltpu.VMEM((len(jobs), lse_count, LANES), jnp.bfloat16),
            pltpu.VMEM((rows, LANES), jnp.float32),
            pltpu.VMEM((rows if is_own else 8, LANES), jnp.float32),
            pltpu.SemaphoreType.DMA((len(jobs), 3)),
        ],
        compiler_params=pltpu.CompilerParams(vmem_limit_bytes=VMEM_LIMIT),
        cost_estimate=pl.CostEstimate(
            flops=2 * pairs * HD, transcendentals=pairs, bytes_accessed=len(jobs) * 2**20
        ),
        name=name,
    )(*arrays, *small)


def job(core_0, core_1, gate=None):
    return (core_0, core_1, gate)


def core_0(role, upper):
    return role == 0


def core_1(role, upper):
    return role == 1


def core_0_upper(role, upper):
    return (role == 0) & upper


def not_core_0_upper(role, upper):
    return (role == 1) | jnp.logical_not(upper)


def finish_far(role, mass, small):
    last_a, middle_a, middle_b = small
    return mass + last_a + jnp.where(role == 1, middle_a + middle_b, 0.0)


def finish_near(role, mass, small):
    own_a, own_b, first_a, middle_a, middle_b = small
    return mass + own_a + own_b + first_a + jnp.where(role == 0, middle_a + middle_b, 0.0)


def move(value, mesh_shape, steps_of_role):
    shards, heads = mesh_shape
    pairs = []
    for shard in range(shards):
        for head in range(heads):
            steps = steps_of_role[head % 2]
            if steps != 0 and 0 <= shard + steps < shards:
                pairs.append((shard * heads + head, (shard + steps) * heads + head))
    return lax.ppermute(value, ("ctx", "head"), pairs)


def move_around(value, mesh_shape):
    shards, heads = mesh_shape
    pairs = []
    for shard in range(shards):
        for head in range(heads):
            if head % 2 == 1 and shard == shards // 2:
                pairs.append((shard * heads + head, head - 1))
            elif head % 2 == 1 and shard > 0:
                pairs.append((shard * heads + head, (shard - 1) * heads + head))
    return lax.ppermute(value, ("ctx", "head"), pairs)


def move_on(value, mesh_shape):
    shards, heads = mesh_shape
    target = shards // 2 - 1
    pairs = [(head, target * heads + head + 1) for head in range(0, heads, 2)]
    return lax.ppermute(value, ("ctx", "head"), pairs)


def after(value, *done):
    return lax.optimization_barrier((value, *done))[0]


def on_device(mesh_shape, key_rows, query_rows, row_lse, query_offsets):
    rows = query_rows.shape[0]
    out, back = (-1, 1), (1, -1)
    xa0, xb0, za0, zb0 = prepare(key_rows, query_rows, row_lse)
    offsets = query_offsets.reshape(rows // LANES, LANES)
    own = [job((0, 1, 0), (1, 0, 0))]
    middle = [job((0, 1, 2), (1, 0, 0))]
    last_relayed = [job((0, 1, 2), ((2, 3), 0, 1))]
    last = [job((0, 1, 2), (1, 0, 1))]
    first_early = [job((0, 1, 1), None, core_0)]
    middle_early = [
        job(None, (1, 0, 0), core_1),
        job((2, 1, 1), None, core_0_upper),
    ]
    near_jobs = [
        job((0, 1, 1), (2, 3, 1), not_core_0_upper),
        job((4, 1, 2), None, core_0),
        job(None, ((5, 6), 7, 1), core_1),
    ]

    xa1 = move(xa0, mesh_shape, out)
    xb1 = move(xb0, mesh_shape, out)
    za1_core_1 = move_around(za0, mesh_shape)
    za1_core_0 = move(za0, mesh_shape, (1, 0))
    own_a = mass_call("own_a", [xa0, za0], own, (offsets,), is_own=True)
    xa1 = after(xa1, own_a)
    xa2 = move(xa1, mesh_shape, out)
    first_a = mass_call("first_a", [xa1, za0], first_early)
    xb1 = after(xb1, first_a)
    xb2 = move(xb1, mesh_shape, out)
    za1_core_1 = after(za1_core_1, xb1)
    za1_relayed = move_on(za1_core_1, mesh_shape)
    zb0 = after(zb0, xb1, za1_core_1)
    zb1 = move(zb0, mesh_shape, back)
    own_b = mass_call("own_b", [after(xb0, za1_core_0), zb0], own, (offsets,), is_own=True)
    middle_a = mass_call("middle_a", [after(xa2, own_b), za0], middle)
    last_a = mass_call(
        "last_a",
        [after(xa2, middle_a), za1_core_0, za1_core_1, za1_relayed],
        last_relayed,
    )
    middle_b = mass_call("middle_b", [xb2, after(zb0, last_a), xb1], middle_early)
    far = mass_call(
        "last_b",
        [xb2, after(zb1, middle_b)],
        last,
        (last_a, middle_a, middle_b),
        finish=finish_far,
    )
    local = mass_call(
        "near",
        [after(xb1, far), zb0, zb1, xb0, xb2, za1_core_1, za1_relayed, xa0],
        near_jobs,
        (own_a, own_b, first_a, middle_a, middle_b),
        finish=finish_near,
    )
    local = local + move(far, mesh_shape, (-1, -2))
    spread = lax.all_to_all(local, "head", 0, 0, tiled=True)
    return jnp.sum(spread, axis=0)


def solution(mesh):
    mesh_shape = (mesh.shape["ctx"], mesh.shape["head"])
    in_specs = (P("ctx", "head"), P("ctx", "head"), P("head", "ctx"), P("ctx"))
    out_specs = P(("ctx", "head"))
    return jax.shard_map(
        functools.partial(on_device, mesh_shape),
        mesh=mesh,
        in_specs=in_specs,
        out_specs=out_specs,
        check_vma=False,
    )
```
